32 devices in a mesh: dp: 4 (over y, x), grp: 8 (over z, core).
Axes of the slice: x: 2, y: 2, z: 4, core: 2. Of those that a mesh axis runs over, the one named last changes fastest.
Arguments:
- tokens: bfloat16 [16384, 768], P(('dp', 'grp')), may hold values from -6 to 6
- cotangent: bfloat16 [16384, 768], P(('dp', 'grp')), may hold values from -6 to 6
- span_order: int32 [4, 8], P('dp'), may hold values from 0 to 7, each once within a row
- input_master: float32 [768, 5376], P('grp'), may hold values from -0.20207259 to 0.20207259
- output_master: float32 [3840, 768], P('grp'), may hold values from -0.5484828 to 0.5484828
- vector_master: float32 [13, 768], P(None, 'grp'), may hold values from -1.2 to 2.6
- input_first: float32 [768, 5376], P('grp'), may hold values from -0.875 to 0.875
- output_first: float32 [3840, 768], P('grp'), may hold values from -0.4375 to 0.4375
- vector_first: float32 [13, 768], P(None, 'grp'), may hold values from -0.875 to 0.875
- input_second: float32 [768, 5376], P('grp'), may hold values from 0.0028217214 to 0.14108607
- output_second: float32 [3840, 768], P('grp'), may hold values from 0.0014108607 to 0.04232582
- vector_second: float32 [13, 768], P(None, 'grp'), may hold values from 0.0028217214 to 0.14108607
Outputs:
- result: bfloat16 [16384, 768], P(('dp', 'grp'))
- token_grad: bfloat16 [16384, 768], P(('dp', 'grp'))
- input_grad: float32 [768, 5376], P('grp')
- output_grad: float32 [3840, 768], P('grp')
- vector_grad: float32 [13, 768], P(None, 'grp')
- input_moment: float32 [768, 5376], P('grp')
- output_moment: float32 [3840, 768], P('grp')
- vector_moment: float32 [13, 768], P(None, 'grp')
- input_updated: float32 [768, 5376], P('grp')
- output_updated: float32 [3840, 768], P('grp')
- vector_updated: float32 [13, 768], P(None, 'grp')
- clip_norm: float32 [], replicated
The draws below stay inside these ranges and needn't reach their ends.
Inputs may be any that keep to these rules, and one draw needn't show every extreme that they name: Each row is a permutation; the device at place g of a group holds span span_order[s, g] of its sequence s.
All inputs are finite; a program needn't handle non-finite values.
Results may differ from the reference program's by a relative error of at most 0.013.
The reference program's roundings to bfloat16 on the way count: a program that leaves them out, or rounds other values in their place, can miss the bound.
Values may be sent and summed in bfloat16 or wider, within the bound.
A program may use at most 256 MiB of HBM per device.

```python
import math
import jax
import jax.numpy as jnp
from jax import lax

D = 768
HEADS = 12
HEAD = 64
ROT = 16
FF = 3072
SPAN = 512
STEP = 10
LENGTH = 4096
SEQUENCES = 4
TOKENS = 16384
PARAMS = 7087872
N_GRP = 8


def draw_input_master(key, part):
    key = jax.random.fold_in(key, 11)
    columns = jnp.arange(3 * D + FF)
    column_scale = jnp.where(columns < 2 * D, 1.4, 1.0) * D ** (-0.5)
    entries = jax.random.truncated_normal(key, -4.0, 4.0, (D, 3 * D + FF), jnp.float32)
    return (entries * column_scale[None, :]).astype(jnp.float32)


def draw_output_master(key, part):
    key = jax.random.fold_in(key, 12)
    row_ids = jnp.arange(D + FF)
    row_scale = jnp.where(row_ids < D, (LENGTH / (400.0 * D)) ** 0.5, 1.2 * FF ** (-0.5))
    entries = jax.random.truncated_normal(key, -4.0, 4.0, (D + FF, D), jnp.float32)
    return (entries * row_scale[:, None]).astype(jnp.float32)


def draw_vector_master(key, part):
    key = jax.random.fold_in(key, 13)
    first_key, second_key = jax.random.split(key)
    fraction = jnp.arange(D, dtype=jnp.float32)[None, :] / D
    row_ids = jnp.arange(13)[:, None]
    is_gain = (row_ids == 0) | (row_ids == 2)
    noise = jax.random.uniform(first_key, (13, D), jnp.float32, 0.8, 1.2)
    gains = (0.5 + fraction) * noise
    others = 0.3 * jax.random.truncated_normal(second_key, -4.0, 4.0, (13, D), jnp.float32)
    return jnp.where(is_gain, gains, others).astype(jnp.float32)


def block_levels(key, extent, cuts, low, largest):
    gain, own = 1.0, jax.random.fold_in(key, 6)
    for axis_at, parts in cuts:
        steps = jnp.exp(jax.random.uniform(jax.random.fold_in(own, axis_at), (parts,), jnp.float32, low / len(cuts), largest / len(cuts)))
        gain = gain * jnp.repeat(steps, extent[axis_at] // parts).reshape([-1 if axis == axis_at else 1 for axis in range(len(extent))])
    return gain


def scatter_about(rng, extent, deviation, reach, shards=(), kind=jnp.bfloat16):
    values = deviation * jax.random.normal(rng, extent, jnp.float32)
    if shards:
        values = values * block_levels(rng, extent, shards, -0.22, 0.18)
    return jnp.clip(values, -reach, reach).astype(kind)


def setup_inputs(seed: int = 0) -> dict:
    splits = jax.random.split(jax.random.key(seed), 13)
    return {
        "tokens": scatter_about(splits[0], (TOKENS, D), 1.0, 6.0, ((0, 32),)),
        "cotangent": scatter_about(splits[1], (TOKENS, D), 1.0, 6.0, ((0, 32),)),
        "span_order": jax.vmap(lambda own: jax.random.permutation(own, N_GRP))(jax.random.split(splits[2], SEQUENCES)).reshape((SEQUENCES, N_GRP)).astype(jnp.int32),
        "input_master": draw_input_master(jax.random.fold_in(splits[12], 71), 0),
        "output_master": draw_output_master(jax.random.fold_in(splits[12], 71), 0),
        "vector_master": draw_vector_master(jax.random.fold_in(splits[12], 71), 0),
        "input_first": scatter_about(splits[6], (D, 3 * D + FF), (150 * PARAMS ** -0.5), 0.875, ((0, 8),), jnp.float32),
        "output_first": scatter_about(splits[7], (D + FF, D), (80 * PARAMS ** -0.5), 0.4375, ((0, 8),), jnp.float32),
        "vector_first": scatter_about(splits[8], (13, D), (150 * PARAMS ** -0.5), 0.875, ((1, 8),), jnp.float32),
        "input_second": jnp.clip(jnp.exp(math.log(0.14108607) - 3.912023 * jax.random.uniform(splits[9], (D, 3 * D + FF), jnp.float32) ** block_levels(splits[9], (D, 3 * D + FF), ((0, 8),), -0.2, 0.2)), 0.0028217214, 0.14108607),
        "output_second": jnp.clip(jnp.exp(math.log(0.04232582) - 3.4011974 * jax.random.uniform(splits[10], (D + FF, D), jnp.float32) ** block_levels(splits[10], (D + FF, D), ((0, 8),), -0.2, 0.2)), 0.0014108607, 0.04232582),
        "vector_second": jnp.clip(jnp.exp(math.log(0.14108607) - 3.912023 * jax.random.uniform(splits[11], (13, D), jnp.float32) ** block_levels(splits[11], (13, D), ((1, 8),), -0.2, 0.2)), 0.0028217214, 0.14108607),
    }


NORM_EPS = 1e-05
ADAM_EPS = 1e-08
BETA_ONE = 0.9
BETA_TWO = 0.95
RATE_MATRIX = 0.06
RATE_VECTOR = 0.6
DECAY_MATRIX = 0.1
CLIP_LIMIT = 1000.0
THETA_BASE = 10000.0
MASKED = -1e+30
ROOT_HALF = 0.7071067811865476

@jax.custom_vjp
def low(v):
    return lax.optimization_barrier(v.astype(jnp.bfloat16)).astype(jnp.float32)

@jax.custom_vjp
def low_back(v):
    return v

def low_keep(v):
    return (low(v), None)

def low_pass(kept, grad):
    return (grad,)

def back_keep(v):
    return (v, None)

def back_low(kept, grad):
    return (low(grad),)
low.defvjp(low_keep, low_pass)
low_back.defvjp(back_keep, back_low)

def matmul(left, right):
    return jnp.dot(left, right, precision=lax.Precision.HIGHEST, preferred_element_type=jnp.float32)

def gelu_exact(inputs):
    return 0.5 * inputs * (1.0 + jax.scipy.special.erf(inputs * ROOT_HALF))

def layer_norm(inputs, gain_row, bias_row):
    center = inputs - lax.optimization_barrier(jnp.mean(inputs, axis=-1, keepdims=True))
    inverse = lax.rsqrt(lax.optimization_barrier(jnp.mean(center * center, axis=-1, keepdims=True)) + NORM_EPS)
    return center * inverse * gain_row + bias_row

def rotate(heads_in, positions):
    half_rot = ROT // 2
    freq_table = THETA_BASE ** (-2.0 * jnp.arange(half_rot, dtype=jnp.float32) / ROT)
    angles = positions[:, None] * freq_table[None, :]
    cosine = jnp.cos(angles)[:, None, :]
    sine_part = jnp.sin(angles)[:, None, :]
    former = heads_in[..., :half_rot]
    latter = heads_in[..., half_rot:ROT]
    return jnp.concatenate([former * cosine - latter * sine_part, latter * cosine + former * sine_part, heads_in[..., ROT:]], axis=-1)

def attention(queries, key_heads, value_heads, positions):
    length = queries.shape[0]
    block_rows = math.gcd(length, 512)
    blocks = length // block_rows
    score_scale = 1.0 / math.sqrt(HEAD)

    def block_fn(block_item):
        query_block, query_pos = block_item
        scores = low_back(jnp.einsum('qhe,khe->hqk', query_block, key_heads, precision=lax.Precision.HIGHEST) * score_scale)
        visible = positions[None, :] <= query_pos[:, None]
        scores = jnp.where(visible[None], scores, MASKED)
        chances = jnp.exp(scores - lax.optimization_barrier(jnp.max(scores, axis=-1, keepdims=True)))
        chances = low(chances / lax.optimization_barrier(jnp.sum(chances, axis=-1, keepdims=True)))
        return jnp.einsum('hqk,khe->qhe', chances, value_heads, precision=lax.Precision.HIGHEST)
    context = lax.map(jax.checkpoint(block_fn), (queries.reshape(blocks, block_rows, HEADS, HEAD), positions.reshape(blocks, block_rows)))
    return context.reshape(length, HEADS, HEAD)

def layer_forward(inputs, weight_in, weight_out, weight_vec, positions):
    length, width = inputs.shape
    attn_in = low(layer_norm(inputs, weight_vec[0], weight_vec[1]))
    feed_in = low(layer_norm(inputs, weight_vec[2], weight_vec[3]))
    projected = low_back(matmul(attn_in, weight_in[:, :3 * width]) + weight_vec[4:7].reshape(-1))
    hidden_pre = low_back(matmul(feed_in, weight_in[:, 3 * width:]) + weight_vec[7:11].reshape(-1))
    queries = low(rotate(projected[:, :width].reshape(length, HEADS, HEAD), positions))
    key_heads = low(rotate(projected[:, width:2 * width].reshape(length, HEADS, HEAD), positions))
    value_heads = low(projected[:, 2 * width:].reshape(length, HEADS, HEAD))
    context = attention(queries, key_heads, value_heads, positions)
    context = low(low_back(context.reshape(length, width)))
    hidden_act = low(gelu_exact(hidden_pre))
    return inputs + matmul(context, weight_out[:width]) + matmul(hidden_act, weight_out[width:]) + weight_vec[11] + weight_vec[12]

def adam_step(master, gradient, moment_one, moment_two, step_rate, decay_rate):
    first_new = BETA_ONE * moment_one + (1.0 - BETA_ONE) * gradient
    second_new = BETA_TWO * moment_two + (1.0 - BETA_TWO) * gradient * gradient
    first_hat = first_new / (1.0 - BETA_ONE ** STEP)
    second_hat = second_new / (1.0 - BETA_TWO ** STEP)
    updated = master - step_rate * (first_hat / (jnp.sqrt(second_hat) + ADAM_EPS) + decay_rate * master)
    return (second_new, updated)

def rounded(array):
    return lax.optimization_barrier(array.astype(jnp.bfloat16)).astype(jnp.float32)

def reference(tokens, cotangent, span_order, input_master, output_master, vector_master, input_first, output_first, vector_first, input_second, output_second, vector_second):
    weight_in = rounded(input_master)
    weight_out = rounded(output_master)
    weight_vec = rounded(vector_master)
    inputs_all = tokens.astype(jnp.float32).reshape(SEQUENCES, LENGTH, D)
    cot_all = cotangent.astype(jnp.float32).reshape(SEQUENCES, LENGTH, D)

    def per_sequence(totals, sequence_item):
        seq_in, seq_cot, order_row = sequence_item
        index = jnp.arange(LENGTH, dtype=jnp.int32)
        positions = (order_row[index // SPAN] * SPAN + index % SPAN).astype(jnp.float32)

        def forward(layer_in, w_first, w_second, w_third):
            return layer_forward(layer_in, w_first, w_second, w_third, positions)
        output, pullback = jax.vjp(forward, seq_in, weight_in, weight_out, weight_vec)
        grad_tokens, grad_in, grad_out, grad_vec = pullback(seq_cot)
        totals = (totals[0] + grad_in, totals[1] + grad_out, totals[2] + grad_vec)
        return (totals, (output.astype(jnp.bfloat16), grad_tokens.astype(jnp.bfloat16)))
    start_totals = (jnp.zeros(input_master.shape, jnp.float32), jnp.zeros(output_master.shape, jnp.float32), jnp.zeros(vector_master.shape, jnp.float32))
    totals, (outputs, token_grads) = lax.scan(per_sequence, start_totals, (inputs_all, cot_all, span_order))
    raw_in, raw_out, raw_vec = totals
    clip_norm = jnp.sqrt(jnp.sum(raw_in * raw_in) + jnp.sum(raw_out * raw_out) + jnp.sum(raw_vec * raw_vec))
    factor = jnp.minimum(1.0, CLIP_LIMIT / (clip_norm + 1e-06))
    input_grad = factor * raw_in
    output_grad = factor * raw_out
    vector_grad = factor * raw_vec
    input_moment, input_updated = adam_step(input_master, input_grad, input_first, input_second, RATE_MATRIX, DECAY_MATRIX)
    output_moment, output_updated = adam_step(output_master, output_grad, output_first, output_second, RATE_MATRIX, DECAY_MATRIX)
    vector_moment, vector_updated = adam_step(vector_master, vector_grad, vector_first, vector_second, RATE_VECTOR, 0.0)
    return (outputs.reshape(TOKENS, D), token_grads.reshape(TOKENS, D), input_grad, output_grad, vector_grad, input_moment, output_moment, vector_moment, input_updated, output_updated, vector_updated, clip_norm)
```

```python
import math

import jax
import jax.numpy as jnp
from jax import lax
from jax.experimental import pallas as pl
from jax.experimental.pallas import tpu as pltpu
from jax.sharding import PartitionSpec as P

HEADS = 12
HEAD = 64
ROT = 16
STEP = 10


NORM_EPS = 1e-05
ADAM_EPS = 1e-08
BETA_ONE = 0.9
BETA_TWO = 0.95
RATE_MATRIX = 0.06
RATE_VECTOR = 0.6
DECAY_MATRIX = 0.1
CLIP_LIMIT = 1000.0
THETA_BASE = 10000.0
MASKED = -1e30
ROOT_HALF = 0.7071067811865476
ROOT_TWOPI = 2.5066282746310002


def gelu_exact(inputs):
    return 0.5 * inputs * (1.0 + jax.scipy.special.erf(inputs * ROOT_HALF))


def gelu_slope(inputs):
    return (
        0.5 * (1.0 + jax.scipy.special.erf(inputs * ROOT_HALF))
        + inputs * jnp.exp(-0.5 * inputs * inputs) / ROOT_TWOPI
    )


def layer_norm(inputs, gain_row, bias_row):
    center = inputs - jnp.mean(inputs, axis=-1, keepdims=True)
    inverse = lax.rsqrt(jnp.mean(center * center, axis=-1, keepdims=True) + NORM_EPS)
    normed = center * inverse
    return (normed * gain_row + bias_row, normed, inverse)


def norm_backward(incoming, normed, inverse, gain_row):
    scaled = incoming * gain_row
    grad_input = inverse * (
        scaled
        - jnp.mean(scaled, axis=-1, keepdims=True)
        - normed * jnp.mean(scaled * normed, axis=-1, keepdims=True)
    )
    return (grad_input, jnp.sum(incoming * normed, axis=0), jnp.sum(incoming, axis=0))


def rotate(heads_in, cosine, sine_part):
    half_rot = ROT // 2
    former = heads_in[:, :half_rot]
    latter = heads_in[:, half_rot:ROT]
    return jnp.concatenate(
        [
            former * cosine - latter * sine_part,
            latter * cosine + former * sine_part,
            heads_in[:, ROT:],
        ],
        axis=1,
    )


def adam_step(master, gradient, moment_one, moment_two, step_rate, decay_rate):
    first_new = BETA_ONE * moment_one + (1.0 - BETA_ONE) * gradient
    second_new = BETA_TWO * moment_two + (1.0 - BETA_TWO) * gradient * gradient
    first_hat = first_new / (1.0 - BETA_ONE**STEP)
    second_hat = second_new / (1.0 - BETA_TWO**STEP)
    updated = master - step_rate * (
        first_hat / (jnp.sqrt(second_hat) + ADAM_EPS) + decay_rate * master
    )
    return (second_new, updated)


def split_alone(heads):
    count, size, rows = heads.shape
    return heads.reshape(count // 3, 3, size, rows)[:, 0::2].reshape(-1, size, rows)


def split_both(heads):
    count, size, rows = heads.shape
    shared = heads.reshape(count // 3, 3, size, rows)[:, 1:2]
    return jnp.broadcast_to(shared, (count // 3, 2, size, rows)).reshape(-1, size, rows)


def fold_half(halves):
    size = halves.shape[1] // 2
    return jnp.concatenate([halves[:, :size], halves[:, size:]], axis=2)


def split_halves(heads):
    count, size, rows = heads.shape
    shared = heads.reshape(count // 3, 3, size, 2, rows // 2)[:, 1]
    return fold_half(shared.transpose(0, 2, 1, 3).reshape(-1, size, rows // 2))


def join_heads(alone, shared):
    devices, size, rows = alone.shape
    pairs = alone.reshape(devices // 2, 2, size, rows)
    return jnp.stack([pairs[:, 0], shared, pairs[:, 1]], axis=1).reshape(-1, size, rows)


def join_halves(packed):
    devices, size, rows = packed.shape
    halves = jnp.concatenate([packed[:, :, : rows // 2], packed[:, :, rows // 2 :]], axis=1)
    halves = halves.reshape(devices // 2, 2, 2 * size, rows // 2).transpose(0, 2, 1, 3)
    return halves.reshape(devices // 2, 2 * size, rows)


def join_both(packed):
    devices, size, rows = packed.shape
    return jnp.sum(packed.astype(jnp.float32).reshape(devices // 2, 2, size, rows), axis=1)


Q_BOTH = HEAD
K_AT = HEAD + HEAD // 2
V_AT = K_AT + 2 * HEAD
PACKED = V_AT + 2 * HEAD


def flip(tile):
    return tile.astype(jnp.float32).T


def take_queries(ref, place, slot):
    if slot == 0:
        return ref[place, :HEAD, :]
    folded = ref[place, Q_BOTH:K_AT, :]
    half = folded.shape[1] // 2
    return jnp.concatenate([folded[:, :half], folded[:, half:]], axis=0)


def visible_mask(keys, count, slot, half):
    key_at = lax.broadcasted_iota(jnp.int32, (keys, count), 0)
    query_at = lax.broadcasted_iota(jnp.int32, (keys, count), 1)
    if slot == 1:
        query_at = query_at + half * count
    return key_at <= query_at


def forward_kernel(span, place_of, half, x_ref, alone_ref, both_ref, la_ref, lb_ref, keys):
    places, _, rows = x_ref.shape

    def stage(place, _):
        for slot in range(2):
            at = K_AT + slot * HEAD
            keys[slot, place] = flip(x_ref[place, at : at + HEAD, :]).astype(jnp.bfloat16)
        return 0

    lax.fori_loop(0, places, stage, 0)
    for slot, (ctx_ref, log_ref) in enumerate(((alone_ref, la_ref), (both_ref, lb_ref))):
        count = ctx_ref.shape[2]
        value_at = V_AT + slot * HEAD

        def work(place, _):
            queries = take_queries(x_ref, place, slot)

            def scores_of(other):
                return jnp.dot(keys[slot, other], queries, preferred_element_type=jnp.float32)

            def weigh(other, weights):
                return jnp.dot(
                    x_ref[other, value_at : value_at + HEAD, :],
                    weights.astype(jnp.bfloat16),
                    preferred_element_type=jnp.float32,
                )

            scores = scores_of(place)
            scores = jnp.where(visible_mask(rows, count, slot, half[0]), scores, MASKED)
            top = jnp.max(scores, axis=0, keepdims=True)
            weights = jnp.exp(scores - top)
            total = jnp.sum(weights, axis=0, keepdims=True)

            def step(index, state):
                context, top, total = state
                other = place_of[index]
                scores = scores_of(other)
                new_top = jnp.maximum(top, jnp.max(scores, axis=0, keepdims=True))
                weights = jnp.exp(scores - new_top)
                factor = jnp.exp(top - new_top)
                total = total * factor + jnp.sum(weights, axis=0, keepdims=True)
                return (context * factor + weigh(other, weights), new_top, total)

            context, top, total = lax.fori_loop(
                0, span[place], step, (weigh(place, weights), top, total)
            )
            ctx_ref[place] = context / total
            log_ref[place] = top + jnp.log(total)
            return 0

        lax.fori_loop(0, places, work, 0)


def backward_kernel(
    span, place_of, half, x_ref, g_ref, alone_ref, both_ref, la_ref, lb_ref,
    out_ref, keys, values, grad_keys, grad_values,
):
    places, _, rows = x_ref.shape

    def stage(place, _):
        for slot in range(2):
            at = K_AT + slot * HEAD
            keys[slot, place] = flip(x_ref[place, at : at + HEAD, :]).astype(jnp.bfloat16)
            at = V_AT + slot * HEAD
            values[slot, place] = flip(x_ref[place, at : at + HEAD, :]).astype(jnp.bfloat16)
            grad_keys[slot, place] = jnp.zeros((rows, HEAD), jnp.float32)
            grad_values[slot, place] = jnp.zeros((rows, HEAD), jnp.float32)
        return 0

    lax.fori_loop(0, places, stage, 0)
    for slot, (ctx_ref, log_ref) in enumerate(((alone_ref, la_ref), (both_ref, lb_ref))):
        count = ctx_ref.shape[2]
        key_at = K_AT + slot * HEAD

        def work(place, _):
            queries = take_queries(x_ref, place, slot)
            grads = take_queries(g_ref, place, slot)
            queries_flat = flip(queries).astype(jnp.bfloat16)
            grads_flat = flip(grads).astype(jnp.bfloat16)
            log_total = log_ref[place]
            row_dot = jnp.sum(grads.astype(jnp.float32) * ctx_ref[place], axis=0, keepdims=True)

            def block(other, masked):
                scores = jnp.dot(keys[slot, other], queries, preferred_element_type=jnp.float32)
                if masked:
                    scores = jnp.where(visible_mask(rows, count, slot, half[0]), scores, MASKED)
                chances = jnp.exp(scores - log_total)
                grad_values[slot, other] += jnp.dot(
                    chances.astype(jnp.bfloat16), grads_flat, preferred_element_type=jnp.float32
                )
                grad_chance = jnp.dot(
                    values[slot, other], grads, preferred_element_type=jnp.float32
                )
                grad_score = (chances * (grad_chance - row_dot)).astype(jnp.bfloat16)
                grad_keys[slot, other] += jnp.dot(
                    grad_score, queries_flat, preferred_element_type=jnp.float32
                )
                return jnp.dot(
                    x_ref[other, key_at : key_at + HEAD, :],
                    grad_score,
                    preferred_element_type=jnp.float32,
                )

            grad_query = lax.fori_loop(
                0,
                span[place],
                lambda index, state: state + block(place_of[index], False),
                block(place, True),
            )
            grad_query = (grad_query * (1.0 / math.sqrt(HEAD))).astype(out_ref.dtype)
            if slot == 0:
                out_ref[place, :HEAD, :] = grad_query
            else:
                out_ref[place, Q_BOTH:K_AT, :] = jnp.concatenate(
                    [grad_query[: HEAD // 2], grad_query[HEAD // 2 :]], axis=1
                )
            return 0

        lax.fori_loop(0, places, work, 0)

    def finish(place, _):
        for slot in range(2):
            at = K_AT + slot * HEAD
            out_ref[place, at : at + HEAD, :] = grad_keys[slot, place].T.astype(out_ref.dtype)
            at = V_AT + slot * HEAD
            out_ref[place, at : at + HEAD, :] = grad_values[slot, place].T.astype(out_ref.dtype)
        return 0

    lax.fori_loop(0, places, finish, 0)


def exchange(packed):
    return lax.all_to_all(packed, "grp", 0, 0, tiled=True)


def local_call(kernel, outputs, scratch, flops, touched, *operands):
    smem = pl.BlockSpec(memory_space=pltpu.SMEM)
    vmem = pl.BlockSpec(memory_space=pltpu.VMEM)
    return pl.pallas_call(
        kernel,
        out_shape=outputs,
        in_specs=[smem] * 3 + [vmem] * (len(operands) - 3),
        out_specs=jax.tree.map(lambda _: vmem, outputs),
        scratch_shapes=scratch,
        compiler_params=pltpu.CompilerParams(vmem_limit_bytes=48 * 1024 * 1024),
        cost_estimate=pl.CostEstimate(
            flops=flops, bytes_accessed=touched, transcendentals=flops // 256
        ),
    )(*operands)


def take_piece(matrix, owner, parts, along):
    piece_size = matrix.shape[along] // parts
    return lax.dynamic_slice_in_dim(matrix, owner * piece_size, piece_size, along)


def square_sum(arrays):
    return sum((jnp.sum(member * member) for member in arrays))


def body(
    tokens,
    cotangent,
    span_order,
    input_master,
    output_master,
    vector_master,
    input_first,
    output_first,
    vector_first,
    input_second,
    output_second,
    vector_second,
):
    width = tokens.shape[1]
    rows_here = tokens.shape[0]
    groups = lax.axis_size("grp")
    score_scale = 1.0 / math.sqrt(HEAD)
    contract_rows = (((0,), (0,)), ((), ()))
    contract_last = (((1,), (1,)), ((), ()))
    flat = (((0,), (1,)), ((), ()))
    f32, bf16 = jnp.float32, jnp.bfloat16

    def gather_rows(shard):
        return lax.all_gather(shard.astype(bf16), "grp", axis=0, tiled=True)

    weight_vec = lax.all_gather(vector_master.astype(bf16), "grp", axis=1, tiled=True)
    weight_attn = gather_rows(input_master[:, : 3 * width])
    weight_ctx = gather_rows(output_master)
    weight_feed = gather_rows(input_master[:, 3 * width :])
    weight_ctx, weight_ffn = weight_ctx[:width], weight_ctx[width:]
    vector_rows = weight_vec.astype(f32)
    inputs = tokens.astype(f32)
    attn_in, normed_one, inverse_one = layer_norm(inputs, vector_rows[0], vector_rows[1])
    attn_in = attn_in.astype(bf16)
    feed_in, normed_two, inverse_two = layer_norm(inputs, vector_rows[2], vector_rows[3])
    feed_in = feed_in.astype(bf16)
    projected = (
        lax.dot_general(weight_attn, attn_in, flat, preferred_element_type=f32)
        + vector_rows[4:7].reshape(-1)[:, None]
    ).reshape(3, HEADS, HEAD, rows_here)
    order_row = span_order[0]
    group_ids = jnp.arange(groups, dtype=jnp.int32)
    place = lax.axis_index("grp")
    own_span = jnp.sum(jnp.where(group_ids == place, order_row, 0))
    place_of = jnp.sum(
        jnp.where(order_row[None, :] == group_ids[:, None], group_ids[None, :], 0), axis=1
    ).astype(jnp.int32)
    half = (place % 2).astype(jnp.int32).reshape(1)
    query_pos = (own_span * rows_here + jnp.arange(rows_here, dtype=jnp.int32)).astype(f32)
    half_rot = ROT // 2
    freq_table = THETA_BASE ** (-2.0 * jnp.arange(half_rot, dtype=f32) / ROT)
    angles = query_pos[None, :] * freq_table[:, None]
    cosine, sine_part = lax.optimization_barrier((jnp.cos(angles), jnp.sin(angles)))
    queries = (rotate(projected[0], cosine, sine_part).astype(bf16) * score_scale).astype(bf16)
    key_heads = rotate(projected[1], cosine, sine_part).astype(bf16)
    value_heads = projected[2].astype(bf16)
    packed = exchange(
        jnp.concatenate(
            [
                split_alone(queries),
                split_halves(queries),
                split_alone(key_heads),
                split_both(key_heads),
                split_alone(value_heads),
                split_both(value_heads),
            ],
            axis=1,
        )
    )
    grad_context = (
        lax.dot_general(weight_ctx, cotangent, contract_last, preferred_element_type=f32)
        .astype(bf16)
        .reshape(HEADS, HEAD, rows_here)
    )
    grad_packed = exchange(
        jnp.concatenate([split_alone(grad_context), split_halves(grad_context)], axis=1)
    )
    tasks = (order_row, place_of, half)
    pair_work = groups * (groups + 1) * 3 * rows_here * rows_here * HEAD
    stage = (2, groups, rows_here, HEAD)
    context_alone, context_both, log_alone, log_both = local_call(
        forward_kernel,
        (
            jax.ShapeDtypeStruct((groups, HEAD, rows_here), f32),
            jax.ShapeDtypeStruct((groups, HEAD, rows_here // 2), f32),
            jax.ShapeDtypeStruct((groups, 1, rows_here), f32),
            jax.ShapeDtypeStruct((groups, 1, rows_here // 2), f32),
        ),
        [pltpu.VMEM(stage, bf16)],
        pair_work * 4,
        packed.size * 4,
        *tasks,
        packed,
    )
    context_back = exchange(
        jnp.concatenate([context_alone, fold_half(context_both)], axis=1).astype(bf16)
    )
    hidden_pre = (
        lax.dot_general(
            feed_in, weight_feed, (((1,), (0,)), ((), ())), preferred_element_type=f32
        )
        + vector_rows[7:11].reshape(-1)
    )
    hidden_act = gelu_exact(hidden_pre).astype(bf16)
    grad_hidden = (
        lax.dot_general(cotangent, weight_ffn, contract_last, preferred_element_type=f32)
        * gelu_slope(hidden_pre)
    ).astype(bf16)

    def scatter_rows(raw):
        return lax.psum_scatter(raw, "grp", scatter_dimension=0, tiled=True)

    def rows_product(left, right):
        return lax.dot_general(left, right, contract_rows, preferred_element_type=f32)

    context_low = join_heads(
        context_back[:, :HEAD], join_halves(context_back[:, HEAD:])
    ).reshape(width, rows_here)
    raw_feed = rows_product(feed_in, grad_hidden).astype(bf16)
    raw_out = jnp.concatenate(
        [
            jnp.dot(context_low, cotangent, preferred_element_type=f32).astype(bf16),
            rows_product(hidden_act, cotangent).astype(bf16),
        ],
        axis=0,
    )
    raw_feed, raw_out, packed, grad_packed = lax.optimization_barrier(
        (raw_feed, raw_out, packed, grad_packed)
    )
    mine_feed, mine_out = scatter_rows(raw_feed), scatter_rows(raw_out)
    sum_feed, sum_out = lax.psum((mine_feed, mine_out), "dp")
    grads_back = exchange(
        local_call(
            backward_kernel,
            jax.ShapeDtypeStruct(packed.shape, bf16),
            [
                pltpu.VMEM(stage, bf16),
                pltpu.VMEM(stage, bf16),
                pltpu.VMEM(stage, f32),
                pltpu.VMEM(stage, f32),
            ],
            pair_work * 10,
            packed.size * 6,
            *tasks,
            packed,
            grad_packed,
            context_alone,
            context_both,
            log_alone,
            log_both,
        )
    )
    result = (
        inputs
        + rows_product(context_low, weight_ctx)
        + jnp.dot(hidden_act, weight_ffn, preferred_element_type=f32)
        + vector_rows[11]
        + vector_rows[12]
    ).astype(bf16)
    back_two = lax.dot_general(
        grad_hidden, weight_feed, contract_last, preferred_element_type=f32
    )
    input_two, gain_two, bias_two = norm_backward(back_two, normed_two, inverse_two, vector_rows[2])
    grad_query = join_heads(
        grads_back[:, :HEAD], join_halves(grads_back[:, Q_BOTH:K_AT])
    ).astype(f32)
    grad_key = join_heads(
        grads_back[:, K_AT : K_AT + HEAD].astype(f32),
        join_both(grads_back[:, K_AT + HEAD : V_AT]),
    )
    grad_value = join_heads(
        grads_back[:, V_AT : V_AT + HEAD].astype(f32),
        join_both(grads_back[:, V_AT + HEAD :]),
    )
    grad_proj = (
        jnp.concatenate(
            [
                rotate(grad_query, cosine, -sine_part),
                rotate(grad_key, cosine, -sine_part),
                grad_value,
            ],
            axis=0,
        )
        .astype(bf16)
        .reshape(3 * width, rows_here)
    )
    raw_attn = lax.dot_general(attn_in, grad_proj, flat, preferred_element_type=f32)
    mine_attn = scatter_rows(raw_attn.astype(bf16))
    mine_attn, sum_feed, sum_out = lax.optimization_barrier((mine_attn, sum_feed, sum_out))
    sum_attn = lax.psum(mine_attn, "dp").astype(f32)
    sum_feed, sum_out = sum_feed.astype(f32), sum_out.astype(f32)
    back_one = lax.dot_general(grad_proj, weight_attn, flat, preferred_element_type=f32)
    input_one, gain_one, bias_one = norm_backward(back_one, normed_one, inverse_one, vector_rows[0])
    token_grad = (cotangent.astype(f32) + input_one + input_two).astype(bf16)
    out_sum = jnp.sum(cotangent, axis=0, dtype=f32)
    raw_vec = jnp.concatenate(
        [
            jnp.stack([gain_one, bias_one, gain_two, bias_two]),
            jnp.sum(grad_proj, axis=1, dtype=f32).reshape(3, width),
            jnp.sum(grad_hidden, axis=0, dtype=f32).reshape(-1, width),
            jnp.stack([out_sum, out_sum]),
        ],
        axis=0,
    )
    vector_sum = lax.psum(raw_vec, ("dp", "grp"))
    matrix_total = lax.psum(square_sum((sum_attn, sum_feed, sum_out)), "grp")
    total = matrix_total + jnp.sum(vector_sum * vector_sum)
    clip_norm = jnp.sqrt(total)
    factor = jnp.minimum(1.0, CLIP_LIMIT / (clip_norm + 1e-06))
    input_grad = factor * jnp.concatenate([sum_attn, sum_feed], axis=1)
    output_grad = factor * sum_out
    vector_grad = factor * take_piece(vector_sum, place, groups, 1)
    input_moment, input_updated = adam_step(
        input_master, input_grad, input_first, input_second, RATE_MATRIX, DECAY_MATRIX
    )
    output_moment, output_updated = adam_step(
        output_master, output_grad, output_first, output_second, RATE_MATRIX, DECAY_MATRIX
    )
    vector_moment, vector_updated = adam_step(
        vector_master, vector_grad, vector_first, vector_second, RATE_VECTOR, 0.0
    )
    return (
        result,
        token_grad,
        input_grad,
        output_grad,
        vector_grad,
        input_moment,
        output_moment,
        vector_moment,
        input_updated,
        output_updated,
        vector_updated,
        clip_norm,
    )


def solution(mesh):
    return jax.shard_map(
        body,
        mesh=mesh,
        in_specs=(
            P(("dp", "grp"), None),
            P(("dp", "grp"), None),
            P("dp", None),
            P("grp", None),
            P("grp", None),
            P(None, "grp"),
            P("grp", None),
            P("grp", None),
            P(None, "grp"),
            P("grp", None),
            P("grp", None),
            P(None, "grp"),
        ),
        out_specs=(
            P(("dp", "grp"), None),
            P(("dp", "grp"), None),
            P("grp", None),
            P("grp", None),
            P(None, "grp"),
            P("grp", None),
            P("grp", None),
            P(None, "grp"),
            P("grp", None),
            P("grp", None),
            P(None, "grp"),
            P(),
        ),
        check_vma=False,
    )
```

```python
import math

import jax
import jax.numpy as jnp
from jax import lax
from jax.experimental import pallas as pl
from jax.experimental.pallas import tpu as pltpu
from jax.sharding import PartitionSpec as P

HEADS = 12
HEAD = 64
ROT = 16
STEP = 10


NORM_EPS = 1e-05
ADAM_EPS = 1e-08
BETA_ONE = 0.9
BETA_TWO = 0.95
RATE_MATRIX = 0.06
RATE_VECTOR = 0.6
DECAY_MATRIX = 0.1
CLIP_LIMIT = 1000.0
THETA_BASE = 10000.0
MASKED = -1e30
ROOT_HALF = 0.7071067811865476
ROOT_TWOPI = 2.5066282746310002


def gelu_exact(inputs):
    return 0.5 * inputs * (1.0 + jax.scipy.special.erf(inputs * ROOT_HALF))


def gelu_slope(inputs):
    return (
        0.5 * (1.0 + jax.scipy.special.erf(inputs * ROOT_HALF))
        + inputs * jnp.exp(-0.5 * inputs * inputs) / ROOT_TWOPI
    )


def layer_norm(inputs, gain_row, bias_row):
    center = inputs - jnp.mean(inputs, axis=-1, keepdims=True)
    inverse = lax.rsqrt(jnp.mean(center * center, axis=-1, keepdims=True) + NORM_EPS)
    normed = center * inverse
    return (normed * gain_row + bias_row, normed, inverse)


def norm_backward(incoming, normed, inverse, gain_row):
    scaled = incoming * gain_row
    grad_input = inverse * (
        scaled
        - jnp.mean(scaled, axis=-1, keepdims=True)
        - normed * jnp.mean(scaled * normed, axis=-1, keepdims=True)
    )
    return (grad_input, jnp.sum(incoming * normed, axis=0), jnp.sum(incoming, axis=0))


def rotate(heads_in, cosine, sine_part):
    half_rot = ROT // 2
    former = heads_in[:, :half_rot]
    latter = heads_in[:, half_rot:ROT]
    return jnp.concatenate(
        [
            former * cosine - latter * sine_part,
            latter * cosine + former * sine_part,
            heads_in[:, ROT:],
        ],
        axis=1,
    )


def adam_step(master, gradient, moment_one, moment_two, step_rate, decay_rate):
    first_new = BETA_ONE * moment_one + (1.0 - BETA_ONE) * gradient
    second_new = BETA_TWO * moment_two + (1.0 - BETA_TWO) * gradient * gradient
    first_hat = first_new / (1.0 - BETA_ONE**STEP)
    second_hat = second_new / (1.0 - BETA_TWO**STEP)
    updated = master - step_rate * (
        first_hat / (jnp.sqrt(second_hat) + ADAM_EPS) + decay_rate * master
    )
    return (second_new, updated)


def split_alone(heads):
    count, size, rows = heads.shape
    return heads.reshape(count // 3, 3, size, rows)[:, 0::2].reshape(-1, size, rows)


def split_both(heads):
    count, size, rows = heads.shape
    shared = heads.reshape(count // 3, 3, size, rows)[:, 1:2]
    return jnp.broadcast_to(shared, (count // 3, 2, size, rows)).reshape(-1, size, rows)


def fold_half(halves):
    size = halves.shape[1] // 2
    return jnp.concatenate([halves[:, :size], halves[:, size:]], axis=2)


def split_halves(heads):
    count, size, rows = heads.shape
    shared = heads.reshape(count // 3, 3, size, 2, rows // 2)[:, 1]
    return fold_half(shared.transpose(0, 2, 1, 3).reshape(-1, size, rows // 2))


def join_heads(alone, shared):
    devices, size, rows = alone.shape
    pairs = alone.reshape(devices // 2, 2, size, rows)
    return jnp.stack([pairs[:, 0], shared, pairs[:, 1]], axis=1).reshape(-1, size, rows)


def join_halves(packed):
    devices, size, rows = packed.shape
    halves = jnp.concatenate([packed[:, :, : rows // 2], packed[:, :, rows // 2 :]], axis=1)
    halves = halves.reshape(devices // 2, 2, 2 * size, rows // 2).transpose(0, 2, 1, 3)
    return halves.reshape(devices // 2, 2 * size, rows)


def join_both(packed):
    devices, size, rows = packed.shape
    return jnp.sum(packed.astype(jnp.float32).reshape(devices // 2, 2, size, rows), axis=1)


Q_BOTH = HEAD
K_AT = HEAD + HEAD // 2
V_AT = K_AT + 2 * HEAD
PACKED = V_AT + 2 * HEAD


def flip(tile):
    return tile.astype(jnp.float32).T


def take_queries(ref, place, slot):
    if slot == 0:
        return ref[place, :HEAD, :]
    folded = ref[place, Q_BOTH:K_AT, :]
    half = folded.shape[1] // 2
    return jnp.concatenate([folded[:, :half], folded[:, half:]], axis=0)


def visible_mask(keys, count, slot, half):
    key_at = lax.broadcasted_iota(jnp.int32, (keys, count), 0)
    query_at = lax.broadcasted_iota(jnp.int32, (keys, count), 1)
    if slot == 1:
        query_at = query_at + half * count
    return key_at <= query_at


def forward_kernel(span, place_of, half, x_ref, alone_ref, both_ref, la_ref, lb_ref, keys):
    places, _, rows = x_ref.shape

    def stage(place, _):
        for slot in range(2):
            at = K_AT + slot * HEAD
            keys[slot, place] = flip(x_ref[place, at : at + HEAD, :]).astype(jnp.bfloat16)
        return 0

    lax.fori_loop(0, places, stage, 0)
    for slot, (ctx_ref, log_ref) in enumerate(((alone_ref, la_ref), (both_ref, lb_ref))):
        count = ctx_ref.shape[2]
        value_at = V_AT + slot * HEAD

        def work(place, _):
            queries = take_queries(x_ref, place, slot)

            def scores_of(other):
                return jnp.dot(keys[slot, other], queries, preferred_element_type=jnp.float32)

            def weigh(other, weights):
                return jnp.dot(
                    x_ref[other, value_at : value_at + HEAD, :],
                    weights.astype(jnp.bfloat16),
                    preferred_element_type=jnp.float32,
                )

            scores = scores_of(place)
            scores = jnp.where(visible_mask(rows, count, slot, half[0]), scores, MASKED)
            top = jnp.max(scores, axis=0, keepdims=True)
            weights = jnp.exp(scores - top)
            total = jnp.sum(weights, axis=0, keepdims=True)

            def step(index, state):
                context, top, total = state
                other = place_of[index]
                scores = scores_of(other)
                new_top = jnp.maximum(top, jnp.max(scores, axis=0, keepdims=True))
                weights = jnp.exp(scores - new_top)
                factor = jnp.exp(top - new_top)
                total = total * factor + jnp.sum(weights, axis=0, keepdims=True)
                return (context * factor + weigh(other, weights), new_top, total)

            context, top, total = lax.fori_loop(
                0, span[place], step, (weigh(place, weights), top, total)
            )
            ctx_ref[place] = context / total
            log_ref[place] = top + jnp.log(total)
            return 0

        lax.fori_loop(0, places, work, 0)


def backward_kernel(
    span, place_of, half, x_ref, g_ref, alone_ref, both_ref, la_ref, lb_ref,
    out_ref, keys, values, grad_keys, grad_values,
):
    places, _, rows = x_ref.shape

    def stage(place, _):
        for slot in range(2):
            at = K_AT + slot * HEAD
            keys[slot, place] = flip(x_ref[place, at : at + HEAD, :]).astype(jnp.bfloat16)
            at = V_AT + slot * HEAD
            values[slot, place] = flip(x_ref[place, at : at + HEAD, :]).astype(jnp.bfloat16)
            grad_keys[slot, place] = jnp.zeros((rows, HEAD), jnp.float32)
            grad_values[slot, place] = jnp.zeros((rows, HEAD), jnp.float32)
        return 0

    lax.fori_loop(0, places, stage, 0)
    for slot, (ctx_ref, log_ref) in enumerate(((alone_ref, la_ref), (both_ref, lb_ref))):
        count = ctx_ref.shape[2]
        key_at = K_AT + slot * HEAD

        def work(place, _):
            queries = take_queries(x_ref, place, slot)
            grads = take_queries(g_ref, place, slot)
            queries_flat = flip(queries).astype(jnp.bfloat16)
            grads_flat = flip(grads).astype(jnp.bfloat16)
            log_total = log_ref[place]
            row_dot = jnp.sum(grads.astype(jnp.float32) * ctx_ref[place], axis=0, keepdims=True)

            def block(other, masked):
                scores = jnp.dot(keys[slot, other], queries, preferred_element_type=jnp.float32)
                if masked:
                    scores = jnp.where(visible_mask(rows, count, slot, half[0]), scores, MASKED)
                chances = jnp.exp(scores - log_total)
                grad_values[slot, other] += jnp.dot(
                    chances.astype(jnp.bfloat16), grads_flat, preferred_element_type=jnp.float32
                )
                grad_chance = jnp.dot(
                    values[slot, other], grads, preferred_element_type=jnp.float32
                )
                grad_score = (chances * (grad_chance - row_dot)).astype(jnp.bfloat16)
                grad_keys[slot, other] += jnp.dot(
                    grad_score, queries_flat, preferred_element_type=jnp.float32
                )
                return jnp.dot(
                    x_ref[other, key_at : key_at + HEAD, :],
                    grad_score,
                    preferred_element_type=jnp.float32,
                )

            grad_query = lax.fori_loop(
                0,
                span[place],
                lambda index, state: state + block(place_of[index], False),
                block(place, True),
            )
            grad_query = (grad_query * (1.0 / math.sqrt(HEAD))).astype(out_ref.dtype)
            if slot == 0:
                out_ref[place, :HEAD, :] = grad_query
            else:
                out_ref[place, Q_BOTH:K_AT, :] = jnp.concatenate(
                    [grad_query[: HEAD // 2], grad_query[HEAD // 2 :]], axis=1
                )
            return 0

        lax.fori_loop(0, places, work, 0)

    def finish(place, _):
        for slot in range(2):
            at = K_AT + slot * HEAD
            out_ref[place, at : at + HEAD, :] = grad_keys[slot, place].T.astype(out_ref.dtype)
            at = V_AT + slot * HEAD
            out_ref[place, at : at + HEAD, :] = grad_values[slot, place].T.astype(out_ref.dtype)
        return 0

    lax.fori_loop(0, places, finish, 0)


def exchange(packed):
    return lax.all_to_all(packed, "grp", 0, 0, tiled=True)


def local_call(kernel, outputs, scratch, flops, touched, *operands):
    smem = pl.BlockSpec(memory_space=pltpu.SMEM)
    vmem = pl.BlockSpec(memory_space=pltpu.VMEM)
    return pl.pallas_call(
        kernel,
        out_shape=outputs,
        in_specs=[smem] * 3 + [vmem] * (len(operands) - 3),
        out_specs=jax.tree.map(lambda _: vmem, outputs),
        scratch_shapes=scratch,
        compiler_params=pltpu.CompilerParams(vmem_limit_bytes=48 * 1024 * 1024),
        cost_estimate=pl.CostEstimate(
            flops=flops, bytes_accessed=touched, transcendentals=flops // 256
        ),
    )(*operands)


def take_piece(matrix, owner, parts, along):
    piece_size = matrix.shape[along] // parts
    return lax.dynamic_slice_in_dim(matrix, owner * piece_size, piece_size, along)


def square_sum(arrays):
    return sum((jnp.sum(member * member) for member in arrays))


def body(
    tokens,
    cotangent,
    span_order,
    input_master,
    output_master,
    vector_master,
    input_first,
    output_first,
    vector_first,
    input_second,
    output_second,
    vector_second,
):
    width = tokens.shape[1]
    rows_here = tokens.shape[0]
    groups = lax.axis_size("grp")
    parts = lax.axis_size("dp")
    score_scale = 1.0 / math.sqrt(HEAD)
    contract_rows = (((0,), (0,)), ((), ()))
    contract_last = (((1,), (1,)), ((), ()))
    flat = (((0,), (1,)), ((), ()))
    f32, bf16 = jnp.float32, jnp.bfloat16

    def gather_rows(shard):
        return lax.all_gather(shard.astype(bf16), "grp", axis=0, tiled=True)

    weight_vec = lax.all_gather(vector_master.astype(bf16), "grp", axis=1, tiled=True)
    weight_attn = gather_rows(input_master[:, : 3 * width])
    weight_ctx = gather_rows(output_master)
    weight_feed = gather_rows(input_master[:, 3 * width :])
    weight_ctx, weight_ffn = weight_ctx[:width], weight_ctx[width:]
    vector_rows = weight_vec.astype(f32)
    inputs = tokens.astype(f32)
    attn_in, normed_one, inverse_one = layer_norm(inputs, vector_rows[0], vector_rows[1])
    attn_in = attn_in.astype(bf16)
    feed_in, normed_two, inverse_two = layer_norm(inputs, vector_rows[2], vector_rows[3])
    feed_in = feed_in.astype(bf16)
    projected = (
        lax.dot_general(weight_attn, attn_in, flat, preferred_element_type=f32)
        + vector_rows[4:7].reshape(-1)[:, None]
    ).reshape(3, HEADS, HEAD, rows_here)
    order_row = span_order[0]
    group_ids = jnp.arange(groups, dtype=jnp.int32)
    place = lax.axis_index("grp")
    own_span = jnp.sum(jnp.where(group_ids == place, order_row, 0))
    place_of = jnp.sum(
        jnp.where(order_row[None, :] == group_ids[:, None], group_ids[None, :], 0), axis=1
    ).astype(jnp.int32)
    half = (place % 2).astype(jnp.int32).reshape(1)
    query_pos = (own_span * rows_here + jnp.arange(rows_here, dtype=jnp.int32)).astype(f32)
    half_rot = ROT // 2
    freq_table = THETA_BASE ** (-2.0 * jnp.arange(half_rot, dtype=f32) / ROT)
    angles = query_pos[None, :] * freq_table[:, None]
    cosine, sine_part = lax.optimization_barrier((jnp.cos(angles), jnp.sin(angles)))
    queries = (rotate(projected[0], cosine, sine_part).astype(bf16) * score_scale).astype(bf16)
    key_heads = rotate(projected[1], cosine, sine_part).astype(bf16)
    value_heads = projected[2].astype(bf16)
    packed = exchange(
        jnp.concatenate(
            [
                split_alone(queries),
                split_halves(queries),
                split_alone(key_heads),
                split_both(key_heads),
                split_alone(value_heads),
                split_both(value_heads),
            ],
            axis=1,
        )
    )
    tasks = (order_row, place_of, half)
    pair_work = groups * (groups + 1) * 3 * rows_here * rows_here * HEAD
    stage = (2, groups, rows_here, HEAD)
    context_alone, context_both, log_alone, log_both = local_call(
        forward_kernel,
        (
            jax.ShapeDtypeStruct((groups, HEAD, rows_here), f32),
            jax.ShapeDtypeStruct((groups, HEAD, rows_here // 2), f32),
            jax.ShapeDtypeStruct((groups, 1, rows_here), f32),
            jax.ShapeDtypeStruct((groups, 1, rows_here // 2), f32),
        ),
        [pltpu.VMEM(stage, bf16)],
        pair_work * 4,
        packed.size * 4,
        *tasks,
        packed,
    )
    context_back = exchange(
        jnp.concatenate([context_alone, fold_half(context_both)], axis=1).astype(bf16)
    )
    weight_ctx, weight_ffn, context_both = lax.optimization_barrier(
        (weight_ctx, weight_ffn, context_both)
    )
    grad_context = (
        lax.dot_general(weight_ctx, cotangent, contract_last, preferred_element_type=f32)
        .astype(bf16)
        .reshape(HEADS, HEAD, rows_here)
    )
    grad_packed = exchange(
        jnp.concatenate([split_alone(grad_context), split_halves(grad_context)], axis=1)
    )
    weight_feed, context_alone = lax.optimization_barrier((weight_feed, context_alone))
    hidden_pre = (
        lax.dot_general(
            feed_in, weight_feed, (((1,), (0,)), ((), ())), preferred_element_type=f32
        )
        + vector_rows[7:11].reshape(-1)
    )
    hidden_act = gelu_exact(hidden_pre).astype(bf16)
    grad_hidden = (
        lax.dot_general(cotangent, weight_ffn, contract_last, preferred_element_type=f32)
        * gelu_slope(hidden_pre)
    ).astype(bf16)

    def order_rows(raw):
        rows, columns = raw.shape
        ordered = raw.reshape(groups, parts, rows // (groups * parts), columns)
        return ordered.transpose(1, 0, 2, 3).reshape(rows, columns)

    def scatter_rows(ordered):
        return lax.psum_scatter(ordered, ("dp", "grp"), scatter_dimension=0, tiled=True)

    def join_rows(mine):
        return lax.all_gather(mine, "dp", axis=0, tiled=True).astype(f32)

    def rows_product(left, right):
        return lax.dot_general(left, right, contract_rows, preferred_element_type=f32)

    context_low = join_heads(
        context_back[:, :HEAD], join_halves(context_back[:, HEAD:])
    ).reshape(width, rows_here)
    raw_feed = rows_product(feed_in, grad_hidden).astype(bf16)
    raw_out = jnp.concatenate(
        [
            jnp.dot(context_low, cotangent, preferred_element_type=f32).astype(bf16),
            rows_product(hidden_act, cotangent).astype(bf16),
        ],
        axis=0,
    )
    raw_feed, raw_out, packed, grad_packed = lax.optimization_barrier(
        (order_rows(raw_feed), order_rows(raw_out), packed, grad_packed)
    )
    mine_out, mine_feed = scatter_rows(raw_out), scatter_rows(raw_feed)
    grads_back = exchange(
        local_call(
            backward_kernel,
            jax.ShapeDtypeStruct(packed.shape, bf16),
            [
                pltpu.VMEM(stage, bf16),
                pltpu.VMEM(stage, bf16),
                pltpu.VMEM(stage, f32),
                pltpu.VMEM(stage, f32),
            ],
            pair_work * 10,
            packed.size * 6,
            *tasks,
            packed,
            grad_packed,
            context_alone,
            context_both,
            log_alone,
            log_both,
        )
    )
    result = (
        inputs
        + rows_product(context_low, weight_ctx)
        + jnp.dot(hidden_act, weight_ffn, preferred_element_type=f32)
        + vector_rows[11]
        + vector_rows[12]
    ).astype(bf16)
    back_two = lax.dot_general(
        grad_hidden, weight_feed, contract_last, preferred_element_type=f32
    )
    input_two, gain_two, bias_two = norm_backward(back_two, normed_two, inverse_two, vector_rows[2])
    grad_query = join_heads(
        grads_back[:, :HEAD], join_halves(grads_back[:, Q_BOTH:K_AT])
    ).astype(f32)
    grad_key = join_heads(
        grads_back[:, K_AT : K_AT + HEAD].astype(f32),
        join_both(grads_back[:, K_AT + HEAD : V_AT]),
    )
    grad_value = join_heads(
        grads_back[:, V_AT : V_AT + HEAD].astype(f32),
        join_both(grads_back[:, V_AT + HEAD :]),
    )
    grad_proj = (
        jnp.concatenate(
            [
                rotate(grad_query, cosine, -sine_part),
                rotate(grad_key, cosine, -sine_part),
                grad_value,
            ],
            axis=0,
        )
        .astype(bf16)
        .reshape(3 * width, rows_here)
    )
    raw_attn = lax.dot_general(attn_in, grad_proj, flat, preferred_element_type=f32)
    raw_attn, mine_out, mine_feed = lax.optimization_barrier(
        (order_rows(raw_attn.astype(bf16)), mine_out, mine_feed)
    )
    mine_attn = scatter_rows(raw_attn)
    back_one = lax.dot_general(grad_proj, weight_attn, flat, preferred_element_type=f32)
    input_one, gain_one, bias_one = norm_backward(back_one, normed_one, inverse_one, vector_rows[0])
    token_grad = (cotangent.astype(f32) + input_one + input_two).astype(bf16)
    out_sum = jnp.sum(cotangent, axis=0, dtype=f32)
    raw_vec = jnp.concatenate(
        [
            jnp.stack([gain_one, bias_one, gain_two, bias_two]),
            jnp.sum(grad_proj, axis=1, dtype=f32).reshape(3, width),
            jnp.sum(grad_hidden, axis=0, dtype=f32).reshape(-1, width),
            jnp.stack([out_sum, out_sum]),
        ],
        axis=0,
    )
    vector_sum = lax.psum(raw_vec, ("dp", "grp"))
    sum_feed, sum_out, sum_attn = join_rows(mine_feed), join_rows(mine_out), join_rows(mine_attn)
    squares = square_sum(tuple(mine.astype(f32) for mine in (mine_attn, mine_feed, mine_out)))
    squares, vector_sum = lax.optimization_barrier((squares, vector_sum))
    matrix_total = lax.psum(squares, ("dp", "grp"))
    total = matrix_total + jnp.sum(vector_sum * vector_sum)
    clip_norm = jnp.sqrt(total)
    factor = jnp.minimum(1.0, CLIP_LIMIT / (clip_norm + 1e-06))
    input_grad = factor * jnp.concatenate([sum_attn, sum_feed], axis=1)
    output_grad = factor * sum_out
    vector_grad = factor * take_piece(vector_sum, place, groups, 1)
    input_moment, input_updated = adam_step(
        input_master, input_grad, input_first, input_second, RATE_MATRIX, DECAY_MATRIX
    )
    output_moment, output_updated = adam_step(
        output_master, output_grad, output_first, output_second, RATE_MATRIX, DECAY_MATRIX
    )
    vector_moment, vector_updated = adam_step(
        vector_master, vector_grad, vector_first, vector_second, RATE_VECTOR, 0.0
    )
    return (
        result,
        token_grad,
        input_grad,
        output_grad,
        vector_grad,
        input_moment,
        output_moment,
        vector_moment,
        input_updated,
        output_updated,
        vector_updated,
        clip_norm,
    )


def solution(mesh):
    return jax.shard_map(
        body,
        mesh=mesh,
        in_specs=(
            P(("dp", "grp"), None),
            P(("dp", "grp"), None),
            P("dp", None),
            P("grp", None),
            P("grp", None),
            P(None, "grp"),
            P("grp", None),
            P("grp", None),
            P(None, "grp"),
            P("grp", None),
            P("grp", None),
            P(None, "grp"),
        ),
        out_specs=(
            P(("dp", "grp"), None),
            P(("dp", "grp"), None),
            P("grp", None),
            P("grp", None),
            P(None, "grp"),
            P("grp", None),
            P("grp", None),
            P(None, "grp"),
            P("grp", None),
            P("grp", None),
            P(None, "grp"),
            P(),
        ),
        check_vma=False,
    )
```
